32 devices in a mesh: dp: 8 (over y, x, core), loop: 4 (over z).
Axes of the slice: x: 2, y: 2, z: 4, core: 2. Of those that a mesh axis runs over, the one named last changes fastest.
Arguments:
- tokens: bfloat16 [1024, 2048], P('dp', 'loop'), may hold values from -6 to 6
- norm_gain: bfloat16 [2048], replicated, may hold values from 0.25 to 1.75
- route_ids: int32 [1024, 8], P('dp'), may hold values from 0 to 127, all different within a row; in each aligned block of 128 rows (0 to 127, 128 to 255, ...) at most 16 rows name the same one
- route_weights: float32 [1024, 8], P('dp'), may hold values from 0.1 to 1
- w_gate: bfloat16 [512, 384, 2048], P(('dp', 'loop')), may hold values from -0.125 to 0.125
- w_up: bfloat16 [512, 384, 2048], P(('dp', 'loop')), may hold values from -0.125 to 0.125
- w_down: bfloat16 [512, 384, 2048], P(('dp', 'loop')), may hold values from -0.15625 to 0.15625
Outputs:
- block_out: bfloat16 [1024, 2048], P('dp', 'loop')
The draws below stay inside these ranges and needn't reach their ends.
Inputs may be any that keep to these rules, and one draw needn't show every extreme that they name: `route_ids`: each row names 8 different experts. Within each aligned block of 128 rows no expert is named by more than 16 rows, and in some blocks an expert is named by exactly 16 rows.
All inputs are finite; a program needn't handle non-finite values.
Results may differ from the reference program's by a relative error of at most 0.0059.
Values may be sent and summed in bfloat16 or wider, within the bound.
A program may use at most 128 MiB of HBM per device.

```python
import math
import jax
import jax.numpy as jnp
import numpy as np
from jax import lax

D = 2048
FF = 1536
EXPERTS = 128
TOP = 8
HGROUPS = 4
R = 128
CAP = 16
TOKENS = 1024
N_DP = 8


def steps_of(own_key, dims, split, low, top_value):
    def one(dim, blocks):
        steps = jax.random.uniform(jax.random.fold_in(jax.random.fold_in(own_key, 6), dim), (blocks,), jnp.float32, low / len(split), top_value / len(split))
        return jnp.repeat(jnp.exp(steps), dims[dim] // blocks).reshape((-1,) + (1,) * (len(dims) - dim - 1))

    level = one(*split[0])
    for cut in split[1:]:
        level = level * one(*cut)
    return level


def routed_block(stream_key, own, number, rows, amount, top, most, skew):
    ranking = jax.random.permutation(stream_key, amount)
    heavy_load, ordinary = portions_of(amount, rows * top, most, skew, True), portions_of(amount, rows * top, most, skew, False)
    places = jnp.arange(amount)

    def named(sizes, turn):
        used = int((sizes > 0).sum())
        fixed = max(1, used // 4)
        moved = fixed + (places - fixed + turn * (used - fixed)) % max(1, amount - fixed)
        return jnp.zeros((amount,), jnp.int32).at[ranking[jnp.where(places < fixed, places, moved)]].set(jnp.asarray(sizes, jnp.int32))

    sizes = jnp.where(number % 4 == 0, named(heavy_load, number // 4), named(ordinary, number - number // 4 - 1))
    mixed = jax.random.permutation(jax.random.fold_in(own, 3), amount)
    donor, taker = mixed[0:amount // 2 * 2:2], mixed[1:amount // 2 * 2:2]
    room = jnp.minimum(sizes[donor] - 1, most - sizes[taker]) // 2
    room = jnp.where((donor == ranking[0]) | (taker == ranking[0]) | (sizes[taker] == 0), 0, jnp.maximum(room, 0))
    moved = jax.random.randint(jax.random.fold_in(own, 4), (amount // 2,), 0, 1 << 20) % (room + 1)
    sizes = sizes.at[donor].add(-moved).at[taker].add(moved)
    labels = jnp.searchsorted(jnp.cumsum(sizes), jnp.arange(rows * top), side="right").astype(jnp.int32)
    listing = labels.reshape(top, rows).T
    listing = listing[jax.random.permutation(jax.random.fold_in(own, 1), rows)]
    turn = jax.random.randint(jax.random.fold_in(own, 2), (rows, 1), 0, top)
    return jnp.take_along_axis(listing, (jnp.arange(top)[None, :] + turn) % top, axis=1)


def portions_of(amount, total, bound, slope, full):
    loads = [(1 << 20) // math.isqrt(grade ** slope) + 1 for grade in range(1, amount + 1)]
    largest = bound if full else min(bound, max(-(-total // amount), total * loads[0] // sum(loads)))
    least = 1 if total - largest >= amount - 1 else 0
    given, spare = [largest] + [least] * (amount - 1), total - largest - least * (amount - 1)
    while spare > 0:
        movable = [i for i in range(1, amount) if given[i] < largest] or [i for i in range(1, amount) if given[i] < bound]
        whole, budget = sum([loads[i] for i in movable]), spare
        for i in movable:
            addition = min(bound - given[i], max(1, budget * loads[i] // whole), spare)
            given[i] = given[i] + addition
            spare = spare - addition
    return np.array(given)


def noise(own_key, dims, scale, bound, cuts=(), kind=jnp.bfloat16):
    values = scale * jax.random.normal(own_key, dims, jnp.float32)
    if cuts:
        values = values * steps_of(own_key, dims, cuts, -0.22, 0.18)
    return jnp.clip(values, -bound, bound).astype(kind)


def setup_inputs(seed: int = 0) -> dict:
    splits = jax.random.split(jax.random.key(seed), 8)
    tokens = noise(splits[0], (TOKENS, D), 1.0, 6.0, ((0, 8), (1, 4)))
    norm_gain = jnp.clip(1.0 + 0.15 * jax.random.normal(splits[1], (D,), jnp.float32), 0.25, 1.75).astype(jnp.bfloat16)
    route_ids_keys = jax.random.split(jax.random.fold_in(splits[2], 1), TOKENS // R)
    route_ids_turns = jax.random.permutation(jax.random.fold_in(splits[2], 3), TOKENS // R)
    route_ids = jax.vmap(lambda own, number: routed_block(jax.random.fold_in(splits[2], 2), own, number, R, EXPERTS, TOP, CAP, 2))(route_ids_keys, route_ids_turns).reshape((TOKENS, TOP))
    route_weights = jnp.clip(jnp.exp(math.log(1.0) - 2.3025851 * jax.random.uniform(splits[3], (TOKENS, TOP), jnp.float32) ** steps_of(splits[3], (TOKENS, TOP), ((0, 8),), -0.2, 0.2)), 0.1, 1.0)
    w_gate = noise(splits[4], (EXPERTS * HGROUPS, FF // HGROUPS, D), D ** -0.5, 0.125, ((0, 32),))
    w_up = noise(splits[5], (EXPERTS * HGROUPS, FF // HGROUPS, D), D ** -0.5, 0.125, ((0, 32),))
    w_down = noise(splits[6], (EXPERTS * HGROUPS, FF // HGROUPS, D), FF ** -0.5, 0.15625, ((0, 32),))
    return dict(tokens=tokens, norm_gain=norm_gain, route_ids=route_ids, route_weights=route_weights, w_gate=w_gate, w_up=w_up, w_down=w_down)


def reference(tokens, norm_gain, route_ids, route_weights, w_gate, w_up, w_down):
    values = tokens.astype(jnp.float32)
    row_scale = lax.rsqrt(lax.optimization_barrier(jnp.mean(values * values, axis=1, keepdims=True)) + 1e-06)
    normed = (values * row_scale * norm_gain.astype(jnp.float32)).astype(jnp.bfloat16)
    per_expert = N_DP * CAP
    flat_ids = route_ids.reshape(-1).astype(jnp.int32)
    onehot = (flat_ids[:, None] == jnp.arange(EXPERTS, dtype=jnp.int32)[None, :]).astype(jnp.int32)
    position = lax.optimization_barrier(jnp.sum((jnp.cumsum(onehot, axis=0) - onehot) * onehot, axis=1)).astype(jnp.int32)
    slot_index = flat_ids * per_expert + position
    pair_ids = jnp.arange(TOKENS * TOP, dtype=jnp.int32)
    slot_owner = jnp.full((EXPERTS * per_expert,), TOKENS, jnp.int32).at[slot_index].set(pair_ids // TOP)
    slot_weight = jnp.zeros((EXPERTS * per_expert,), jnp.float32).at[slot_index].set(route_weights.reshape(-1).astype(jnp.float32))
    slot_owner = slot_owner.reshape(EXPERTS, per_expert)
    slot_weight = slot_weight.reshape(EXPERTS, per_expert)
    padded = jnp.concatenate([normed, jnp.zeros((1, D), jnp.bfloat16)], axis=0)
    group_width = FF // HGROUPS

    def expert_step(total, item):
        gate_w, up_w, down_w, rows_idx, row_w = item
        batch = padded[rows_idx]
        gate_part = jnp.dot(batch, gate_w.T, preferred_element_type=jnp.float32)
        up_part = jnp.dot(batch, up_w.T, preferred_element_type=jnp.float32)
        hidden = (jax.nn.silu(gate_part) * up_part).astype(jnp.bfloat16)
        expert_parts = jnp.einsum('rsf,sfd->srd', hidden.reshape(per_expert, HGROUPS, group_width).astype(jnp.float32), down_w.reshape(HGROUPS, group_width, D).astype(jnp.float32), precision=lax.Precision.HIGHEST)
        rounded = lax.optimization_barrier(expert_parts.astype(jnp.bfloat16))
        contrib = lax.optimization_barrier(jnp.sum(rounded.astype(jnp.float32), axis=0)) * row_w[:, None]
        return (total.at[rows_idx].add(contrib), None)
    start = jnp.zeros((TOKENS + 1, D), jnp.float32)
    items = (w_gate.reshape(EXPERTS, FF, D), w_up.reshape(EXPERTS, FF, D), w_down.reshape(EXPERTS, FF, D), slot_owner, slot_weight)
    total, unused = lax.scan(expert_step, start, items)
    return (values + total[:TOKENS]).astype(jnp.bfloat16)
```

```python
import functools

import jax
import jax.numpy as jnp
from jax import lax
from jax.experimental import pallas as pl
from jax.experimental.pallas import tpu as pltpu
from jax.sharding import PartitionSpec as P

HGROUPS = 4
CAP = 16
SLOTS = 8
COLUMNS = 512
MESH = pl.DeviceIdType.MESH


def kernel(
    sizes,
    tokens_ref,
    gain_ref,
    ids_ref,
    factor_ref,
    gate_hbm,
    up_hbm,
    down_hbm,
    out_ref,
    full,
    normed,
    place,
    mix_high,
    mix_low,
    outgoing,
    arrived,
    hidden,
    results,
    returned,
    partial,
    landed,
    gate_buf,
    up_buf,
    down_buf,
    gate_sem,
    up_sem,
    down_sem,
    row_send,
    row_recv,
    go_send,
    go_recv,
    back_send,
    back_recv,
    part_send,
    part_recv,
):
    groups, loops, own, per, slots = sizes
    pairs = own * per
    rows, width = tokens_ref.shape
    full_width = loops * width
    block = groups * CAP
    top = ids_ref.shape[1]
    mine = lax.axis_index("dp")
    spot = lax.axis_index("loop")

    def gate_copy(pair):
        slot = lax.rem(pair, slots)
        return pltpu.make_async_copy(gate_hbm.at[pair], gate_buf.at[slot], gate_sem.at[slot])

    def up_copy(pair):
        slot = lax.rem(pair, slots)
        return pltpu.make_async_copy(up_hbm.at[pair], up_buf.at[slot], up_sem.at[slot])

    def down_copy(pair):
        slot = lax.rem(pair, slots)
        return pltpu.make_async_copy(down_hbm.at[pair], down_buf.at[slot], down_sem.at[slot])

    def row_copy(owner, target):
        return pltpu.make_async_remote_copy(
            src_ref=tokens_ref,
            dst_ref=full.at[owner],
            send_sem=row_send.at[target],
            recv_sem=row_recv.at[owner],
            device_id=(mine, target),
            device_id_type=MESH,
        )

    def go_copy(expert, owner, target):
        return pltpu.make_async_remote_copy(
            src_ref=outgoing.at[expert, target],
            dst_ref=arrived.at[expert, owner],
            send_sem=go_send.at[expert, target],
            recv_sem=go_recv.at[expert, owner],
            device_id=(target, spot),
            device_id_type=MESH,
        )

    def back_copy(expert, owner, target):
        return pltpu.make_async_remote_copy(
            src_ref=results.at[expert, target],
            dst_ref=returned.at[expert, owner],
            send_sem=back_send.at[expert, target],
            recv_sem=back_recv.at[expert, owner],
            device_id=(target, spot),
            device_id_type=MESH,
        )

    def part_copy(owner, target):
        return pltpu.make_async_remote_copy(
            src_ref=partial.at[target],
            dst_ref=landed.at[owner],
            send_sem=part_send.at[target],
            recv_sem=part_recv.at[owner],
            device_id=(mine, target),
            device_id_type=MESH,
        )

    def loop_peers(body):
        def step(i, carry):
            body(lax.rem(spot + i, loops))
            return carry

        lax.fori_loop(1, loops, step, 0)

    def dp_peers(body):
        def step(i, carry):
            body(lax.rem(mine + i, groups))
            return carry

        lax.fori_loop(1, groups, step, 0)

    barrier = pltpu.get_barrier_semaphore()
    loop_peers(
        lambda peer: pl.semaphore_signal(
            barrier, inc=1, device_id=(mine, peer), device_id_type=MESH
        )
    )
    dp_peers(
        lambda peer: pl.semaphore_signal(
            barrier, inc=1, device_id=(peer, spot), device_id_type=MESH
        )
    )
    pl.semaphore_wait(barrier, loops + groups - 2)
    loop_peers(lambda peer: row_copy(spot, peer).start())

    def prefetch(pair, carry):
        gate_copy(pair).start()
        up_copy(pair).start()
        down_copy(pair).start()
        return carry

    lax.fori_loop(0, slots, prefetch, 0)

    total_slots = own * block
    column = lax.broadcasted_iota(jnp.int32, (rows, total_slots), 1)
    owner = lax.rem(column, block) // CAP
    first = spot * pairs // HGROUPS
    expert_of = owner * (pairs * loops // HGROUPS) + first + column // block
    chosen = jnp.zeros((rows, total_slots), jnp.float32)
    factor = jnp.zeros((rows, total_slots), jnp.float32)
    for k in range(top):
        hit = ids_ref[:, k : k + 1] == expert_of
        chosen = jnp.where(hit, 1.0, chosen)
        factor = jnp.where(hit, factor_ref[:, k : k + 1], factor)
    earlier = (
        lax.broadcasted_iota(jnp.int32, (rows, rows), 1)
        < lax.broadcasted_iota(jnp.int32, (rows, rows), 0)
    ).astype(jnp.float32)
    rank = jnp.dot(
        earlier.astype(jnp.bfloat16),
        chosen.astype(jnp.bfloat16),
        preferred_element_type=jnp.float32,
    )
    here = jnp.where(rank == lax.rem(column, CAP).astype(jnp.float32), chosen, 0.0)
    factor = factor * here
    high = factor.astype(jnp.bfloat16)
    place[...] = here.astype(jnp.bfloat16)
    mix_high[...] = high
    mix_low[...] = (factor - high.astype(jnp.float32)).astype(jnp.bfloat16)

    full[spot] = tokens_ref[...]
    loop_peers(lambda peer: row_copy(peer, peer).wait_recv())
    square = jnp.zeros((rows, 1), jnp.float32)
    for j in range(loops):
        values = full[j].astype(jnp.float32)
        square = square + jnp.sum(values * values, axis=1, keepdims=True)
    row_scale = lax.rsqrt(square / full_width + 1e-06)
    for j in range(loops):
        columns = pl.ds(j * width, width)
        gain = gain_ref[:, columns].astype(jnp.float32)
        normed[:, columns] = (full[j].astype(jnp.float32) * row_scale * gain).astype(jnp.bfloat16)

    for o in range(own):
        picked = lax.dot_general(
            place[:, o * block : (o + 1) * block],
            normed[...],
            (((0,), (0,)), ((), ())),
            preferred_element_type=jnp.float32,
        ).astype(jnp.bfloat16)
        outgoing[o] = picked.reshape(groups, CAP, full_width)
        dp_peers(lambda peer: go_copy(o, mine, peer).start())
        arrived[o, mine] = outgoing[o, mine]

    def expert_step(o, carry):
        dp_peers(lambda peer: go_copy(o, peer, peer).wait_recv())

        def pair_step(h, inner):
            pair = o * per + h
            slot = lax.rem(pair, slots)
            batch = arrived[o].reshape(block, full_width)
            gate_copy(pair).wait()
            up_copy(pair).wait()
            contract = (((1,), (1,)), ((), ()))
            gate = lax.dot_general(
                batch, gate_buf[slot], contract, preferred_element_type=jnp.float32
            )
            up = lax.dot_general(batch, up_buf[slot], contract, preferred_element_type=jnp.float32)
            hidden[h] = (gate / (1.0 + jnp.exp(-gate)) * up).astype(jnp.bfloat16)

            @pl.when(pair + slots < pairs)
            def _():
                gate_copy(pair + slots).start()
                up_copy(pair + slots).start()

            return inner

        lax.fori_loop(0, per, pair_step, 0)
        for h in range(per):
            down_copy(o * per + h).wait()
        for c in range(full_width // COLUMNS):
            columns = pl.ds(c * COLUMNS, COLUMNS)
            total = None
            for h in range(per):
                slot = lax.rem(o * per + h, slots)
                term = jnp.dot(
                    hidden[h], down_buf[slot, :, columns], preferred_element_type=jnp.float32
                )
                total = term if total is None else total + term
            results[o, :, :, columns] = total.astype(jnp.bfloat16).reshape(groups, CAP, COLUMNS)
        for h in range(per):

            @pl.when(o * per + h + slots < pairs)
            def _():
                down_copy(o * per + h + slots).start()

        dp_peers(lambda peer: back_copy(o, mine, peer).start())
        returned[o, mine] = results[o, mine]
        return carry

    lax.fori_loop(0, own, expert_step, 0)

    def expert_wait(o, carry):
        dp_peers(lambda peer: back_copy(o, peer, peer).wait_recv())
        return carry

    lax.fori_loop(0, own, expert_wait, 0)
    for j in range(loops):
        columns = pl.ds(j * width, width)
        rows_back = returned[:, :, :, columns].reshape(total_slots, width)
        mixed = jnp.dot(mix_high[...], rows_back, preferred_element_type=jnp.float32)
        mixed = mixed + jnp.dot(mix_low[...], rows_back, preferred_element_type=jnp.float32)
        partial[j] = mixed.astype(jnp.bfloat16)

        @pl.when(spot != j)
        def _():
            part_copy(spot, j).start()

    landed[spot] = partial[spot]
    loop_peers(lambda peer: part_copy(peer, peer).wait_recv())
    total = tokens_ref[...].astype(jnp.float32)
    for j in range(loops):
        total = total + landed[j].astype(jnp.float32)
    out_ref[...] = total.astype(out_ref.dtype)

    loop_peers(lambda peer: row_copy(spot, peer).wait_send())
    loop_peers(lambda peer: part_copy(spot, peer).wait_send())

    def drain(o, carry):
        dp_peers(lambda peer: go_copy(o, mine, peer).wait_send())
        dp_peers(lambda peer: back_copy(o, mine, peer).wait_send())
        return carry

    lax.fori_loop(0, own, drain, 0)


def shards(tokens, norm_gain, route_ids, route_weights, w_gate, w_up, w_down):
    rows, width = tokens.shape
    groups, loops = lax.axis_size("dp"), lax.axis_size("loop")
    pairs, hidden_width, full_width = w_gate.shape
    own = max(1, pairs // HGROUPS)
    per = pairs // own
    slots = min(SLOTS, pairs)
    block = groups * CAP
    half, single = jnp.bfloat16, jnp.float32
    vmem = pl.BlockSpec(memory_space=pltpu.VMEM)
    anywhere = pl.BlockSpec(memory_space=pl.ANY)
    dma = pltpu.SemaphoreType.DMA
    weights = pltpu.VMEM((slots, hidden_width, full_width), half)
    exchange = pltpu.VMEM((own, groups, CAP, full_width), half)
    return pl.pallas_call(
        functools.partial(kernel, (groups, loops, own, per, slots)),
        out_shape=jax.ShapeDtypeStruct((rows, width), half),
        in_specs=[vmem] * 4 + [anywhere] * 3,
        out_specs=vmem,
        scratch_shapes=[
            pltpu.VMEM((loops, rows, width), half),
            pltpu.VMEM((rows, full_width), half),
            pltpu.VMEM((rows, own * block), half),
            pltpu.VMEM((rows, own * block), half),
            pltpu.VMEM((rows, own * block), half),
            exchange,
            exchange,
            pltpu.VMEM((per, block, hidden_width), half),
            exchange,
            exchange,
            pltpu.VMEM((loops, rows, width), half),
            pltpu.VMEM((loops, rows, width), half),
            weights,
            weights,
            weights,
            dma((slots,)),
            dma((slots,)),
            dma((slots,)),
            dma((loops,)),
            dma((loops,)),
            dma((own, groups)),
            dma((own, groups)),
            dma((own, groups)),
            dma((own, groups)),
            dma((loops,)),
            dma((loops,)),
        ],
        compiler_params=pltpu.CompilerParams(
            collective_id=0, has_side_effects=True, vmem_limit_bytes=60 * 1024 * 1024
        ),
        cost_estimate=pl.CostEstimate(
            flops=6 * pairs * block * hidden_width * full_width,
            bytes_accessed=6 * pairs * hidden_width * full_width,
            transcendentals=pairs * block * hidden_width,
        ),
    )(tokens, norm_gain.reshape(1, full_width), route_ids, route_weights, w_gate, w_up, w_down)


def solution(mesh):
    return jax.shard_map(
        shards,
        mesh=mesh,
        in_specs=(
            P("dp", "loop"),
            P(),
            P("dp", None),
            P("dp", None),
            P(("dp", "loop"), None, None),
            P(("dp", "loop"), None, None),
            P(("dp", "loop"), None, None),
        ),
        out_specs=P("dp", "loop"),
        check_vma=False,
    )
```

```python
import functools

import jax
import jax.numpy as jnp
from jax import lax
from jax.experimental import pallas as pl
from jax.experimental.pallas import tpu as pltpu
from jax.sharding import PartitionSpec as P

HGROUPS = 4
CAP = 16
SLOTS = 8
PIECES = 4
MESH = pl.DeviceIdType.MESH


def kernel(
    sizes,
    tokens_ref,
    gain_ref,
    ids_ref,
    factor_ref,
    gate_hbm,
    up_hbm,
    down_hbm,
    out_ref,
    full,
    batch,
    place,
    mix_high,
    mix_low,
    near_out,
    near,
    far_out,
    far,
    hidden,
    results,
    returned,
    partial,
    landed,
    gate_buf,
    up_buf,
    down_buf,
    gate_sem,
    up_sem,
    down_sem,
    row_send,
    row_recv,
    near_send,
    near_recv,
    far_send,
    far_recv,
    back_send,
    back_recv,
    piece_send,
    piece_recv,
    part_send,
    part_recv,
):
    groups, loops, own, per, slots = sizes
    pairs = own * per
    rows, width = tokens_ref.shape
    full_width = loops * width
    block = groups * CAP
    top = ids_ref.shape[1]
    pieces = min(PIECES, loops)
    share = loops // pieces
    mine = lax.axis_index("dp")
    spot = lax.axis_index("loop")

    def gate_copy(pair):
        slot = lax.rem(pair, slots)
        return pltpu.make_async_copy(gate_hbm.at[pair], gate_buf.at[slot], gate_sem.at[slot])

    def up_copy(pair):
        slot = lax.rem(pair, slots)
        return pltpu.make_async_copy(up_hbm.at[pair], up_buf.at[slot], up_sem.at[slot])

    def down_copy(pair):
        slot = lax.rem(pair, slots)
        return pltpu.make_async_copy(down_hbm.at[pair], down_buf.at[slot], down_sem.at[slot])

    def row_copy(owner, target):
        return pltpu.make_async_remote_copy(
            src_ref=tokens_ref,
            dst_ref=full.at[owner],
            send_sem=row_send.at[target],
            recv_sem=row_recv.at[owner],
            device_id=(mine, target),
            device_id_type=MESH,
        )

    def near_copy(owner, target):
        return pltpu.make_async_remote_copy(
            src_ref=near_out.at[target],
            dst_ref=near.at[owner],
            send_sem=near_send.at[target],
            recv_sem=near_recv.at[owner],
            device_id=(target, spot),
            device_id_type=MESH,
        )

    def far_copy(expert, owner, target):
        return pltpu.make_async_remote_copy(
            src_ref=far_out.at[expert, target],
            dst_ref=far.at[expert, owner],
            send_sem=far_send.at[expert, target],
            recv_sem=far_recv.at[expert, owner],
            device_id=(target, spot),
            device_id_type=MESH,
        )

    def back_copy(expert, owner, target):
        return pltpu.make_async_remote_copy(
            src_ref=results.at[expert, target],
            dst_ref=returned.at[expert, owner],
            send_sem=back_send.at[expert, target],
            recv_sem=back_recv.at[expert, owner],
            device_id=(target, spot),
            device_id_type=MESH,
        )

    def piece_columns(c):
        piece = lax.rem(spot // share + 1 + c, pieces)
        return pl.ds(pl.multiple_of(piece * share * width, share * width), share * width)

    def piece_copy(c, owner, target):
        return pltpu.make_async_remote_copy(
            src_ref=results.at[own - 1, target, :, piece_columns(c)],
            dst_ref=returned.at[own - 1, owner, :, piece_columns(c)],
            send_sem=piece_send.at[c, target],
            recv_sem=piece_recv.at[c, owner],
            device_id=(target, spot),
            device_id_type=MESH,
        )

    def part_copy(owner, target):
        return pltpu.make_async_remote_copy(
            src_ref=partial.at[target],
            dst_ref=landed.at[owner],
            send_sem=part_send.at[target],
            recv_sem=part_recv.at[owner],
            device_id=(mine, target),
            device_id_type=MESH,
        )

    def loop_peers(body):
        def step(i, carry):
            body(lax.rem(spot + i, loops))
            return carry

        lax.fori_loop(1, loops, step, 0)

    def dp_peers(body):
        def step(i, carry):
            body(lax.rem(mine + i, groups))
            return carry

        lax.fori_loop(1, groups, step, 0)

    barrier = pltpu.get_barrier_semaphore()
    loop_peers(
        lambda peer: pl.semaphore_signal(
            barrier, inc=1, device_id=(mine, peer), device_id_type=MESH
        )
    )
    dp_peers(
        lambda peer: pl.semaphore_signal(
            barrier, inc=1, device_id=(peer, spot), device_id_type=MESH
        )
    )

    def prefetch(pair, carry):
        gate_copy(pair).start()
        up_copy(pair).start()
        down_copy(pair).start()
        return carry

    lax.fori_loop(0, slots, prefetch, 0)

    total_slots = own * block
    column = lax.broadcasted_iota(jnp.int32, (rows, total_slots), 1)
    owner = lax.rem(column, block) // CAP
    first = spot * pairs // HGROUPS
    expert_of = owner * (pairs * loops // HGROUPS) + first + column // block
    chosen = jnp.zeros((rows, total_slots), jnp.float32)
    factor = jnp.zeros((rows, total_slots), jnp.float32)
    for k in range(top):
        hit = ids_ref[:, k : k + 1] == expert_of
        chosen = jnp.where(hit, 1.0, chosen)
        factor = jnp.where(hit, factor_ref[:, k : k + 1], factor)
    earlier = (
        lax.broadcasted_iota(jnp.int32, (rows, rows), 1)
        < lax.broadcasted_iota(jnp.int32, (rows, rows), 0)
    ).astype(jnp.float32)
    rank = jnp.dot(
        earlier.astype(jnp.bfloat16),
        chosen.astype(jnp.bfloat16),
        preferred_element_type=jnp.float32,
    )
    here = jnp.where(rank == lax.rem(column, CAP).astype(jnp.float32), chosen, 0.0)
    factor = factor * here
    high = factor.astype(jnp.bfloat16)
    place[...] = here.astype(jnp.bfloat16)
    mix_high[...] = high
    mix_low[...] = (factor - high.astype(jnp.float32)).astype(jnp.bfloat16)

    gathering = (((0,), (0,)), ((), ()))
    picked = lax.dot_general(
        place[...], tokens_ref[...], gathering, preferred_element_type=jnp.float32
    ).astype(jnp.bfloat16)
    picked = picked.reshape(own, groups, CAP, width)
    for o in range(own):
        near_out[:, o] = picked[o]
    pl.semaphore_wait(barrier, loops + groups - 2)
    loop_peers(lambda peer: row_copy(spot, peer).start())
    dp_peers(lambda peer: near_copy(mine, peer).start())
    near[mine] = near_out[mine]

    loop_peers(lambda peer: row_copy(peer, peer).wait_recv())
    for o in range(own):
        for i in range(1, loops):
            picked = lax.dot_general(
                place[:, o * block : (o + 1) * block],
                full[lax.rem(spot + i, loops)],
                gathering,
                preferred_element_type=jnp.float32,
            ).astype(jnp.bfloat16)
            far_out[o, :, i - 1] = picked.reshape(groups, CAP, width)
        dp_peers(lambda peer: far_copy(o, mine, peer).start())
        far[o, mine] = far_out[o, mine]

    dp_peers(lambda peer: near_copy(peer, peer).wait_recv())

    def expert_step(o, carry):
        dp_peers(lambda peer: far_copy(o, peer, peer).wait_recv())
        square = jnp.zeros((block, 1), jnp.float32)
        for i in range(loops):
            raw = near[:, o] if i == 0 else far[o, :, i - 1]
            values = raw.reshape(block, width).astype(jnp.float32)
            square = square + jnp.sum(values * values, axis=1, keepdims=True)
        row_scale = lax.rsqrt(square / full_width + 1e-06)
        for i in range(loops):
            raw = near[:, o] if i == 0 else far[o, :, i - 1]
            values = raw.reshape(block, width).astype(jnp.float32)
            columns = pl.ds(pl.multiple_of(lax.rem(spot + i, loops) * width, width), width)
            gain = gain_ref[:, columns].astype(jnp.float32)
            batch[:, columns] = (values * row_scale * gain).astype(jnp.bfloat16)

        def pair_step(h, inner):
            pair = o * per + h
            slot = lax.rem(pair, slots)
            normed = batch[...]
            gate_copy(pair).wait()
            up_copy(pair).wait()
            contract = (((1,), (1,)), ((), ()))
            gate = lax.dot_general(
                normed, gate_buf[slot], contract, preferred_element_type=jnp.float32
            )
            up = lax.dot_general(normed, up_buf[slot], contract, preferred_element_type=jnp.float32)
            hidden[h] = (gate / (1.0 + jnp.exp(-gate)) * up).astype(jnp.bfloat16)

            @pl.when(pair + slots < pairs)
            def _():
                gate_copy(pair + slots).start()
                up_copy(pair + slots).start()

            return inner

        lax.fori_loop(0, per, pair_step, 0)
        for h in range(per):
            down_copy(o * per + h).wait()
        for c in range(pieces):
            columns = piece_columns(c)
            total = None
            for h in range(per):
                slot = lax.rem(o * per + h, slots)
                term = jnp.dot(
                    hidden[h], down_buf[slot, :, columns], preferred_element_type=jnp.float32
                )
                total = term if total is None else total + term
            results[o, :, :, columns] = total.astype(jnp.bfloat16).reshape(
                groups, CAP, share * width
            )

            @pl.when(o == own - 1)
            def _():
                dp_peers(lambda peer: piece_copy(c, mine, peer).start())

        for h in range(per):

            @pl.when(o * per + h + slots < pairs)
            def _():
                down_copy(o * per + h + slots).start()

        @pl.when(o < own - 1)
        def _():
            dp_peers(lambda peer: back_copy(o, mine, peer).start())

        returned[o, mine] = results[o, mine]
        return carry

    lax.fori_loop(0, own, expert_step, 0)

    def expert_wait(o, carry):
        dp_peers(lambda peer: back_copy(o, peer, peer).wait_recv())
        return carry

    lax.fori_loop(0, own - 1, expert_wait, 0)
    for c in range(pieces):
        dp_peers(lambda peer: piece_copy(c, peer, peer).wait_recv())
        for i in range(share):
            target = lax.rem(spot // share + 1 + c, pieces) * share + i
            columns = pl.ds(pl.multiple_of(target * width, width), width)
            rows_back = returned[:, :, :, columns].reshape(total_slots, width)
            mixed = jnp.dot(mix_high[...], rows_back, preferred_element_type=jnp.float32)
            mixed = mixed + jnp.dot(mix_low[...], rows_back, preferred_element_type=jnp.float32)
            partial[target] = mixed.astype(jnp.bfloat16)

            @pl.when(target != spot)
            def _():
                part_copy(spot, target).start()

    landed[spot] = partial[spot]
    loop_peers(lambda peer: part_copy(peer, peer).wait_recv())
    total = tokens_ref[...].astype(jnp.float32)
    for j in range(loops):
        total = total + landed[j].astype(jnp.float32)
    out_ref[...] = total.astype(out_ref.dtype)

    loop_peers(lambda peer: row_copy(spot, peer).wait_send())
    loop_peers(lambda peer: part_copy(spot, peer).wait_send())

    dp_peers(lambda peer: near_copy(mine, peer).wait_send())

    def drain_far(o, carry):
        dp_peers(lambda peer: far_copy(o, mine, peer).wait_send())
        return carry

    def drain_back(o, carry):
        dp_peers(lambda peer: back_copy(o, mine, peer).wait_send())
        return carry

    lax.fori_loop(0, own, drain_far, 0)
    lax.fori_loop(0, own - 1, drain_back, 0)
    for c in range(pieces):
        dp_peers(lambda peer: piece_copy(c, mine, peer).wait_send())


def shards(tokens, norm_gain, route_ids, route_weights, w_gate, w_up, w_down):
    rows, width = tokens.shape
    groups, loops = lax.axis_size("dp"), lax.axis_size("loop")
    pairs, hidden_width, full_width = w_gate.shape
    own = max(1, pairs // HGROUPS)
    per = pairs // own
    slots = min(SLOTS, pairs)
    pieces = min(PIECES, loops)
    block = groups * CAP
    half, single = jnp.bfloat16, jnp.float32
    vmem = pl.BlockSpec(memory_space=pltpu.VMEM)
    anywhere = pl.BlockSpec(memory_space=pl.ANY)
    dma = pltpu.SemaphoreType.DMA
    weights = pltpu.VMEM((slots, hidden_width, full_width), half)
    near = pltpu.VMEM((groups, own, CAP, width), half)
    far = pltpu.VMEM((own, groups, loops - 1, CAP, width), half)
    exchange = pltpu.VMEM((own, groups, CAP, full_width), half)
    return pl.pallas_call(
        functools.partial(kernel, (groups, loops, own, per, slots)),
        out_shape=jax.ShapeDtypeStruct((rows, width), half),
        in_specs=[vmem] * 4 + [anywhere] * 3,
        out_specs=vmem,
        scratch_shapes=[
            pltpu.VMEM((loops, rows, width), half),
            pltpu.VMEM((block, full_width), half),
            pltpu.VMEM((rows, own * block), half),
            pltpu.VMEM((rows, own * block), half),
            pltpu.VMEM((rows, own * block), half),
            near,
            near,
            far,
            far,
            pltpu.VMEM((per, block, hidden_width), half),
            exchange,
            exchange,
            pltpu.VMEM((loops, rows, width), half),
            pltpu.VMEM((loops, rows, width), half),
            weights,
            weights,
            weights,
            dma((slots,)),
            dma((slots,)),
            dma((slots,)),
            dma((loops,)),
            dma((loops,)),
            dma((groups,)),
            dma((groups,)),
            dma((own, groups)),
            dma((own, groups)),
            dma((own, groups)),
            dma((own, groups)),
            dma((pieces, groups)),
            dma((pieces, groups)),
            dma((loops,)),
            dma((loops,)),
        ],
        compiler_params=pltpu.CompilerParams(
            collective_id=0, has_side_effects=True, vmem_limit_bytes=60 * 1024 * 1024
        ),
        cost_estimate=pl.CostEstimate(
            flops=6 * pairs * block * hidden_width * full_width,
            bytes_accessed=6 * pairs * hidden_width * full_width,
            transcendentals=pairs * block * hidden_width,
        ),
    )(tokens, norm_gain.reshape(1, full_width), route_ids, route_weights, w_gate, w_up, w_down)


def solution(mesh):
    return jax.shard_map(
        shards,
        mesh=mesh,
        in_specs=(
            P("dp", "loop"),
            P(),
            P("dp", None),
            P("dp", None),
            P(("dp", "loop"), None, None),
            P(("dp", "loop"), None, None),
            P(("dp", "loop"), None, None),
        ),
        out_specs=P("dp", "loop"),
        check_vma=False,
    )
```
